32 devices in a mesh: groups: 2 (over y), tm: 16 (over z, x, core).
Axes of the slice: x: 2, y: 2, z: 4, core: 2. Of those that a mesh axis runs over, the one named last changes fastest.
Arguments:
- observations: float32 [32, 128], P(('groups', 'tm')), parts along dimension 0, may hold values from -6 to 6
- noise_var: float32 [32, 128], P(('groups', 'tm')), parts along dimension 0, may hold values from 0.05 to 2
- gauge_index: int32 [256], P('groups'), parts along dimension 0, may hold values from 0 to 255, as said below
- dynamics: float32 [256, 256], replicated
- process: float32 [256, 256], replicated
Outputs:
- filtered: float32 [32, 256], P(('groups', 'tm')), parts along dimension 0
- filtered_cov: float32 [32, 256, 256], P(('groups', 'tm')), parts along dimension 0
- smoothed: float32 [32, 256], P(('groups', 'tm')), parts along dimension 0
The draws below stay inside these ranges and needn't reach their ends.
There are 2 independent parts, one for each index of `groups`. The reference program is written for one: setup_inputs(seed, part) draws one part's arguments, and reference() takes and returns one part's arrays. A program takes and returns all parts, laid end to end along the dimension named above; an argument that names none is the same for every part. Nothing has to cross between parts.
Inputs may be any that keep to these rules, and one draw needn't show every extreme that they name: `gauge_index`: the 128 numbers are distinct.
All inputs are finite; a program needn't handle non-finite values.
Results may differ from the reference program's by a relative error of at most 0.00015.
Values sent between devices are 32-bit elements; how exact they have to be, the bound alone decides.
A program may use at most 256 MiB of HBM per device.

```python
import math
import jax
import jax.numpy as jnp
from jax import lax

STATE = 256
GAUGE = 128
STEPS = 16


def draw_gauge_index(key, part):
    key = jax.random.fold_in(key, 11)
    shuffle_key, order_key = jax.random.split(key)
    inner_states = 1 + jax.random.permutation(shuffle_key, STATE - 2)[:GAUGE - 2]
    picked = jnp.concatenate([jnp.array([0, STATE - 1], dtype=jnp.int32), inner_states.astype(jnp.int32)])
    return jax.random.permutation(order_key, picked).astype(jnp.int32)


def draw_dynamics(key, part):
    key = jax.random.fold_in(key, 23)
    diag_key, coupling_key = jax.random.split(key)
    diagonal = jnp.exp(jax.random.uniform(diag_key, (STATE,), jnp.float32, math.log(0.4), math.log(0.97)))
    coupling = jax.random.uniform(coupling_key, (STATE, STATE), jnp.float32, -0.016, 0.016)
    identity = jnp.eye(STATE, dtype=jnp.float32)
    return coupling * (1.0 - identity) + identity * diagonal[None, :]


def draw_process(key, part):
    key = jax.random.fold_in(key, 37)
    diag_key, coupling_key = jax.random.split(key)
    variances = jnp.exp(jax.random.uniform(diag_key, (STATE,), jnp.float32, math.log(0.7), math.log(1.6)))
    raw_noise = jax.random.uniform(coupling_key, (STATE, STATE), jnp.float32, -0.034, 0.034)
    symmetric = 0.5 * (raw_noise + raw_noise.T)
    identity = jnp.eye(STATE, dtype=jnp.float32)
    return symmetric * (1.0 - identity) + identity * variances[None, :]


def shard_levels(key, extent, cuts, low, largest):
    def one(axis_at, shards_of):
        draws = jax.random.uniform(jax.random.fold_in(jax.random.fold_in(key, 6), axis_at), (shards_of,), jnp.float32, low / len(cuts), largest / len(cuts))
        return jnp.repeat(jnp.exp(draws), extent[axis_at] // shards_of).reshape((-1,) + (1,) * (len(extent) - axis_at - 1))

    factor_of = one(*cuts[0])
    for cut in cuts[1:]:
        factor_of = factor_of * one(*cut)
    return factor_of


def noise(key, shape, width, bound, pieces=(), kind=jnp.bfloat16):
    drawn = jax.random.normal(key, shape, jnp.float32) * width
    if len(pieces) > 0:
        drawn = shard_levels(key, shape, pieces, -0.22, 0.18) * drawn
    return jnp.clip(drawn, min=-bound, max=bound).astype(kind)


def setup_inputs(seed: int = 0, part: int = 0) -> dict:
    streams_of = jax.random.split(jax.random.key(seed), 6)
    part_keys = jax.random.split(jax.random.fold_in(streams_of[5], part), 6)
    observations = noise(part_keys[0], (STEPS, GAUGE), 1.0, 6.0, ((0, 16),), jnp.float32)
    noise_var = jnp.clip(jnp.exp(math.log(2.0) - 3.6888794 * jax.random.uniform(part_keys[1], (STEPS, GAUGE), jnp.float32) ** shard_levels(part_keys[1], (STEPS, GAUGE), ((0, 16),), -0.2, 0.2)), 0.05, 2.0)
    gauge_index = draw_gauge_index(jax.random.fold_in(jax.random.fold_in(streams_of[5], part), 71), part)
    dynamics = draw_dynamics(jax.random.fold_in(streams_of[5], 71), part)
    process = draw_process(jax.random.fold_in(streams_of[5], 71), part)
    return {"observations": observations, "noise_var": noise_var, "gauge_index": gauge_index, "dynamics": dynamics, "process": process}


HIGHEST = lax.Precision.HIGHEST

def matmul(left, right):
    return jnp.matmul(left, right, precision=HIGHEST)

def chol_solve(factor, rhs):
    column = rhs.ndim == 1
    block_rhs = rhs[:, None] if column else rhs
    half_solved = lax.linalg.triangular_solve(factor, block_rhs, left_side=True, lower=True)
    full_solved = lax.linalg.triangular_solve(factor, half_solved, left_side=True, lower=True, transpose_a=True)
    return full_solved[:, 0] if column else full_solved

def selector_matrix(gauge_index, states):
    return (gauge_index[:, None] == jnp.arange(states, dtype=jnp.int32)[None, :]).astype(jnp.float32)

def filter_step(carried, inputs, selector, dynamics, process):
    state_mean, state_cov = carried
    obs_row, var_row = inputs
    pred_mean = matmul(dynamics, state_mean)
    pred_cov = matmul(matmul(dynamics, state_cov), dynamics.T) + process
    sel_cov = matmul(selector, pred_cov)
    innovation = matmul(sel_cov, selector.T) + jnp.diag(var_row)
    factor = jnp.linalg.cholesky(innovation)
    solved = chol_solve(factor, sel_cov)
    residual = obs_row - matmul(selector, pred_mean)
    new_mean = pred_mean + matmul(solved.T, residual)
    new_cov = pred_cov - matmul(sel_cov.T, solved)
    return ((new_mean, new_cov), (new_mean, new_cov))

def smoother_gain(state_cov, dynamics, process):
    propagated = matmul(dynamics, state_cov)
    predicted = matmul(propagated, dynamics.T) + process
    factor = jnp.linalg.cholesky(predicted)
    return chol_solve(factor, propagated).T

def reference(observations, noise_var, gauge_index, dynamics, process):
    selector = selector_matrix(gauge_index, STATE)

    def advance(carried, inputs):
        return filter_step(carried, inputs, selector, dynamics, process)
    start = (jnp.zeros((STATE,), jnp.float32), jnp.zeros((STATE, STATE), jnp.float32))
    final_state, outputs = lax.scan(advance, start, (observations, noise_var))
    filtered_means, filtered_covs = outputs
    gains = lax.map(lambda one_cov: smoother_gain(one_cov, dynamics, process), filtered_covs)
    position = jnp.arange(STEPS, dtype=jnp.int32)
    keep_gain = 1.0 - (position == STEPS - 1).astype(jnp.float32)
    gains = gains * keep_gain[:, None, None]
    moved_means = jnp.einsum('ij,tj->ti', dynamics, filtered_means, precision=HIGHEST)
    offsets = filtered_means - jnp.einsum('tij,tj->ti', gains, moved_means, precision=HIGHEST)

    def retreat(carried, inputs):
        step_gain, step_offset = inputs
        smoothed_now = matmul(step_gain, carried) + step_offset
        return (smoothed_now, smoothed_now)
    final_value, smoothed = lax.scan(retreat, jnp.zeros((STATE,), jnp.float32), (gains, offsets), reverse=True)
    return (filtered_means, filtered_covs, smoothed)
```

```python
import functools

import jax
import jax.numpy as jnp
from jax import lax
from jax.experimental import pallas as pl
from jax.experimental.pallas import tpu as pltpu
from jax.sharding import PartitionSpec as P

F32 = jnp.float32
BF16 = jnp.bfloat16
HIGHEST = lax.Precision.HIGHEST
RESIDUAL_LIMIT = 1e-4


def split(a):
    high = a.astype(BF16)
    return high, (a - high.astype(F32)).astype(BF16)


def dot(a, b):
    return jnp.dot(a, b, preferred_element_type=F32)


def dot3(a, b):
    (ah, al), (bh, bl) = a, b
    return dot(
        jnp.concatenate([ah, ah, al], axis=1), jnp.concatenate([bh, bl, bh], axis=0)
    )


def dot_t(a, b):
    return lax.dot_general(a, b, (((1,), (1,)), ((), ())), preferred_element_type=F32)


def full(a, b):
    return jnp.dot(a, b, precision=HIGHEST, preferred_element_type=F32)


def iotas(shape):
    return (
        lax.broadcasted_iota(jnp.int32, shape, 0),
        lax.broadcasted_iota(jnp.int32, shape, 1),
    )


def permutation(index_row, states, gauges):
    rows, cols = iotas((states, gauges))
    gauged = (rows == index_row).astype(F32)
    free = 1.0 - jnp.sum(gauged, axis=1, keepdims=True)
    r, c = iotas((states, states))
    below = (c < r).astype(F32)
    rank = dot(below, jnp.broadcast_to(free, (states, gauges)))
    others = jnp.where(rank == cols.astype(F32), free, 0.0)
    return jnp.concatenate([gauged, others], axis=1)


def kernel(
    steps,
    gathered_ref,
    index_ref,
    dynamics_ref,
    process_ref,
    filtered_ref,
    cov_ref,
    smoothed_ref,
    f_ref,
    fh_ref,
    ft_ref,
    q_ref,
    perm_ref,
    pred_ref,
    gain_ref,
    resid_ref,
    kept_ref,
    kept_rows_ref,
    work_ref,
):
    states = dynamics_ref.shape[0]
    gauges = index_ref.shape[1]
    me = lax.axis_index("tm")
    rg, cg = iotas((gauges, gauges))
    eye = (rg == cg).astype(F32)

    perm_t = permutation(index_ref[...], states, gauges)
    perm = perm_t.T
    perm_ref[...] = perm
    f = full(full(perm, dynamics_ref[...]), perm_t)
    f_ref[...] = f
    ft = f.T
    ft_h, ft_l = split(ft)
    ft_ref[0], ft_ref[1] = ft_h, ft_l
    f_h, f_l = split(f)
    fh_ref[0], fh_ref[1] = f_h, f_l
    q_ref[...] = full(full(perm, process_ref[...]), perm_t)

    def gauss_jordan(s):
        work_ref[...] = s

        def pivot(k, nothing):
            m = work_ref[...]
            row = jnp.sum(jnp.where(rg == k, m, 0.0), axis=0, keepdims=True)
            col = jnp.sum(jnp.where(cg == k, m, 0.0), axis=1, keepdims=True)
            inv = 1.0 / jnp.sum(jnp.where(cg[:1] == k, row, 0.0), axis=1, keepdims=True)
            scaled = row * inv
            new = m - col * scaled
            new = jnp.where(cg == k, -col * inv, new)
            new_row = jnp.where(cg[:1] == k, inv, scaled)
            work_ref[...] = jnp.where(rg == k, new_row, new)
            return nothing

        lax.fori_loop(0, gauges, pivot, 0)
        return work_ref[...]

    def run(robust):
        mm = full if robust else (lambda a, b: dot3(split(a), split(b)))
        pred_ref[...] = q_ref[...]

        def forward(t, carried):
            x, worst = carried
            obs = gathered_ref[t][:, :gauges]
            r_row = gathered_ref[t][:, gauges:]
            r_col = jnp.sum(eye * r_row, axis=1, keepdims=True)
            s = pred_ref[:gauges, :gauges] + eye * r_row
            diag = eye * s
            d_row = lax.rsqrt(jnp.sum(diag, axis=0, keepdims=True))
            d_col = lax.rsqrt(jnp.sum(diag, axis=1, keepdims=True))
            scaled = s * d_col * d_row
            b = d_col * pred_ref[:gauges, gauges:]
            if robust:
                inverse = gauss_jordan(scaled)
                both = jnp.concatenate([inverse, full(inverse, b)], axis=1)
            else:
                e = eye - scaled
                e1 = e.astype(BF16)
                e2 = dot(e1, e1)
                e2b = e2.astype(BF16)
                e34 = dot(e2b, jnp.concatenate([e1, e2b], axis=1))
                y3 = eye + e + e2 + e34[:, :gauges]
                x7 = y3 + dot(e34[:, gauges:].astype(BF16), y3.astype(BF16))
                xs = split(x7)
                prod = dot3(xs, split(jnp.concatenate([e, b], axis=1)))
                residual = eye - x7 + prod[:, :gauges]
                half = prod[:, gauges:]
                both = jnp.concatenate([x7, half], axis=1) + dot(
                    residual.astype(BF16),
                    jnp.concatenate([xs[0], half.astype(BF16)], axis=1),
                )
                worst = jnp.maximum(
                    worst, jnp.sum(residual * residual, axis=0, keepdims=True)
                )
            w = both[:, :gauges] * d_col * d_row
            vt = both[:, gauges:] * d_col
            gain = jnp.concatenate([w, vt], axis=1)
            gain_ref[t] = gain
            y = obs - x[:, :gauges]
            resid_ref[t] = y
            gy = mm(jnp.broadcast_to(y, (8, gauges)), gain)[:1]
            mean = jnp.concatenate(
                [obs - r_row * gy[:, :gauges], x[:, gauges:] + gy[:, gauges:]], axis=1
            )
            p_ou = vt * r_col
            p_oo = eye * r_row - w * r_col * r_row
            p_uu = pred_ref[gauges:, gauges:] - mm(pred_ref[gauges:, :gauges], vt)
            cov = jnp.concatenate(
                [
                    jnp.concatenate([p_oo, p_ou], axis=1),
                    jnp.concatenate([p_ou.T, p_uu], axis=1),
                ],
                axis=0,
            )
            slot = jnp.where(t == me, 0, 1)
            kept_ref[slot] = cov
            kept_rows_ref[slot] = jnp.broadcast_to(mean, (8, states))
            stacked = jnp.concatenate([cov, jnp.broadcast_to(mean, (16, states))], axis=0)
            if robust:
                moved = full(stacked, f_ref[...].T)
                pred_ref[...] = full(f_ref[...], moved[:states]) + q_ref[...]
            else:
                moved = dot3(split(stacked), (ft_ref[0], ft_ref[1]))
                pred_ref[...] = (
                    dot3((fh_ref[0], fh_ref[1]), split(moved[:states])) + q_ref[...]
                )
            return moved[states : states + 1], worst

        zero = jnp.zeros((1, states), F32)
        nothing, worst = lax.fori_loop(
            0, steps, forward, (zero, jnp.zeros((1, gauges), F32))
        )

        def backward(i, lam):
            t = steps - 1 - i
            slot = jnp.where(t == me, 2, 3)
            kept_rows_ref[slot] = jnp.broadcast_to(lam, (8, states))
            r_row = gathered_ref[t][:, gauges:]
            y = resid_ref[t]
            z = jnp.concatenate([r_row * lam[:, :gauges] - y, -lam[:, gauges:]], axis=1)
            z = jnp.broadcast_to(z, (8, states))
            if robust:
                new = full(z, gain_ref[t].T)[:1]
            else:
                zh, zl = split(z)
                gh, gl = split(gain_ref[t])
                new = (dot_t(zh, gh) + (dot_t(zh, gl) + dot_t(zl, gh)))[:1]
            joined = jnp.broadcast_to(
                jnp.concatenate([new, lam[:, gauges:]], axis=1), (8, states)
            )
            if robust:
                return full(joined, f_ref[...])[:1]
            return dot3(split(joined), (fh_ref[0], fh_ref[1]))[:1]

        lax.fori_loop(0, steps, backward, zero)
        return jnp.sum(worst)

    worst = run(False)

    @pl.when(jnp.logical_not(worst < RESIDUAL_LIMIT))
    def _():
        run(True)

    perm = perm_ref[...]
    cov = kept_ref[0]
    cov_ref[0] = full(full(perm.T, cov), perm)
    mean, lam = kept_rows_ref[0], kept_rows_ref[2]
    smooth = mean - full(lam, cov)
    filtered_ref[...] = full(mean, perm)[:1]
    smoothed_ref[...] = full(smooth, perm)[:1]


def shards(observations, noise_var, gauge_index, dynamics, process):
    states = dynamics.shape[0]
    gauges = gauge_index.shape[0]
    packed = jnp.concatenate([observations, noise_var], axis=1)
    gathered = lax.all_gather(packed, "tm")
    steps = gathered.shape[0]
    vmem = pl.BlockSpec(memory_space=pltpu.VMEM)
    return pl.pallas_call(
        functools.partial(kernel, steps),
        out_shape=(
            jax.ShapeDtypeStruct((1, states), F32),
            jax.ShapeDtypeStruct((1, states, states), F32),
            jax.ShapeDtypeStruct((1, states), F32),
        ),
        in_specs=[vmem] * 4,
        out_specs=(vmem,) * 3,
        scratch_shapes=[
            pltpu.VMEM((states, states), F32),
            pltpu.VMEM((2, states, states), BF16),
            pltpu.VMEM((2, states, states), BF16),
            pltpu.VMEM((states, states), F32),
            pltpu.VMEM((states, states), F32),
            pltpu.VMEM((states, states), F32),
            pltpu.VMEM((steps, gauges, states), F32),
            pltpu.VMEM((steps, 1, gauges), F32),
            pltpu.VMEM((2, states, states), F32),
            pltpu.VMEM((4, 8, states), F32),
            pltpu.VMEM((gauges, gauges), F32),
        ],
        compiler_params=pltpu.CompilerParams(vmem_limit_bytes=48 * 1024 * 1024),
    )(gathered, gauge_index.reshape(1, gauges), dynamics, process)


def solution(mesh):
    return jax.shard_map(
        shards,
        mesh=mesh,
        in_specs=(P(("groups", "tm"), None), P(("groups", "tm"), None), P("groups"), P(), P()),
        out_specs=(
            P(("groups", "tm"), None),
            P(("groups", "tm"), None, None),
            P(("groups", "tm"), None),
        ),
        check_vma=False,
    )
```

```python
import functools

import jax
import jax.numpy as jnp
import numpy as np
from jax import lax
from jax.experimental import pallas as pl
from jax.experimental.pallas import tpu as pltpu
from jax.sharding import PartitionSpec as P

F32 = jnp.float32
BF16 = jnp.bfloat16
HIGHEST = lax.Precision.HIGHEST
MESH = pl.DeviceIdType.MESH
RADIUS = 0.3
HALF_DEGREE = 4
RESIDUAL_LIMIT = 1e-6


def split(a):
    high = a.astype(BF16)
    return high, (a - high.astype(F32)).astype(BF16)


def dot(a, b):
    return jnp.dot(a, b, preferred_element_type=F32)


def dot3(a, b):
    (ah, al), (bh, bl) = a, b
    return dot(
        jnp.concatenate([ah, ah, al], axis=1), jnp.concatenate([bh, bl, bh], axis=0)
    )


def dot_t(a, b):
    return lax.dot_general(a, b, (((1,), (1,)), ((), ())), preferred_element_type=F32)


def full(a, b):
    return jnp.dot(a, b, precision=HIGHEST, preferred_element_type=F32)


def iotas(shape):
    return (
        lax.broadcasted_iota(jnp.int32, shape, 0),
        lax.broadcasted_iota(jnp.int32, shape, 1),
    )


def permutation(index_row, states, gauges):
    rows, cols = iotas((states, gauges))
    gauged = (rows == index_row).astype(F32)
    free = 1.0 - jnp.sum(gauged, axis=1, keepdims=True)
    r, c = iotas((states, states))
    below = (c < r).astype(F32)
    rank = dot(below, jnp.broadcast_to(free, (states, gauges)))
    others = jnp.where(rank == cols.astype(F32), free, 0.0)
    return jnp.concatenate([gauged, others], axis=1)


def dot3_t(a, b):
    (ah, al), (bh, bl) = a, b
    return dot_t(jnp.concatenate([ah, ah, al], axis=1), jnp.concatenate([bh, bl, bh], axis=1))


def move(a, b):
    if a.dtype == BF16:
        high, low = split(b)
        return dot(a, high) + dot(a, low)
    high, low = split(a)
    return dot(high, b) + dot(low, b)


def factors():
    degree = 2 * HALF_DEGREE
    z = 1.0 / RADIUS
    u = [np.poly1d([1.0]), np.poly1d([2.0, 0.0])]
    for _ in range(degree):
        u.append(np.poly1d([2.0, 0.0]) * u[-1] - u[-2])
    rest = sum((k(z) * k for k in u), np.poly1d([0.0])) / sum(k(z) ** 2 for k in u)
    scaled = np.poly1d([c * z ** (len(rest.coeffs) - 1 - i) for i, c in enumerate(rest.coeffs)])
    quotient, _ = np.polydiv((np.poly1d([1.0]) - scaled).coeffs, np.array([-1.0, 1.0]))
    roots = sorted(np.roots(quotient), key=lambda r: (abs(r.imag) < 1e-9, r.real, r.imag))
    pick = [r for i, r in enumerate(roots) if (i // 2) % 2 == 0]
    other = [r for i, r in enumerate(roots) if (i // 2) % 2 == 1]
    first = np.real(np.poly(pick))
    first = first / first[-1]
    second = np.real(np.poly(other))
    second = second / second[-1] * quotient[-1]
    return [float(c) for c in first[::-1]], [float(c) for c in second[::-1]]


def gather_kernel(count, obs_ref, var_ref, out_ref, row_ref, send_sem, recv_sem):
    me = lax.axis_index("tm")
    group = lax.axis_index("groups")
    gauges = obs_ref.shape[1]
    barrier = pltpu.get_barrier_semaphore()

    def greet(d, nothing):
        peer = lax.rem(me + d, count)
        pl.semaphore_signal(barrier, inc=1, device_id=(group, peer), device_id_type=MESH)
        return nothing

    lax.fori_loop(1, count, greet, 0)
    row_ref[0, :, :gauges] = obs_ref[...]
    row_ref[0, :, gauges:] = var_ref[...]
    out_ref[me] = row_ref[0]
    pl.semaphore_wait(barrier, count - 1)

    def copy(d):
        peer = lax.rem(me + d, count)
        return pltpu.make_async_remote_copy(
            src_ref=row_ref.at[0],
            dst_ref=out_ref.at[me],
            send_sem=send_sem.at[d],
            recv_sem=recv_sem.at[d],
            device_id=(group, peer),
            device_id_type=MESH,
        )

    def start(d, nothing):
        copy(d).start()
        return nothing

    def finish(d, nothing):
        copy(d).wait()
        return nothing

    lax.fori_loop(1, count, start, 0)
    lax.fori_loop(1, count, finish, 0)


def kernel(
    steps,
    gathered_ref,
    index_ref,
    dynamics_ref,
    process_ref,
    filtered_ref,
    cov_ref,
    smoothed_ref,
    f_ref,
    ft_ref,
    q_ref,
    perm_ref,
    perm_t_ref,
    pred_ref,
    gain_ref,
    poly_ref,
    rows_ref,
    kept_ref,
    kept_gain_ref,
    kept_rows_ref,
    work_ref,
):
    states = dynamics_ref.shape[0]
    gauges = index_ref.shape[1]
    me = lax.axis_index("tm")
    rg, cg = iotas((gauges, gauges))
    eye = (rg == cg).astype(F32)
    first, second = factors()

    perm_t = permutation(index_ref[...], states, gauges)
    perm = perm_t.T.astype(BF16)
    perm_t = perm_t.astype(BF16)
    perm_ref[...] = perm
    perm_t_ref[...] = perm_t
    f = move(move(perm, dynamics_ref[...]), perm_t)
    f_ref[0], f_ref[1] = split(f)
    ft_ref[0], ft_ref[1] = split(f.T)
    q_ref[...] = move(move(perm, process_ref[...]), perm_t)

    def gauss_jordan(s):
        work_ref[...] = s

        def pivot(k, nothing):
            m = work_ref[...]
            row = jnp.sum(jnp.where(rg == k, m, 0.0), axis=0, keepdims=True)
            col = jnp.sum(jnp.where(cg == k, m, 0.0), axis=1, keepdims=True)
            inv = 1.0 / jnp.sum(jnp.where(cg[:1] == k, row, 0.0), axis=1, keepdims=True)
            scaled = row * inv
            new = m - col * scaled
            new = jnp.where(cg == k, -col * inv, new)
            new_row = jnp.where(cg[:1] == k, inv, scaled)
            work_ref[...] = jnp.where(rg == k, new_row, new)
            return nothing

        lax.fori_loop(0, gauges, pivot, 0)
        return work_ref[...]

    def step_rows(t):
        row = gathered_ref[t]
        return row[:, :gauges], row[:, gauges:]

    def mean_step(t, x, y):
        g = split(gain_ref[t])
        moved = dot3(split(jnp.broadcast_to(x, (16, states))), (ft_ref[0], ft_ref[1]))
        gy = dot3(split(jnp.broadcast_to(y, (16, gauges))), g)
        rows_ref[t] = gy[:1, :gauges]
        return moved[:1] + gy[:1, gauges:]

    def run(robust):
        pred_ref[...] = q_ref[...]
        gain_ref[0] = jnp.zeros_like(gain_ref[0])

        def forward(t, carried):
            x, y = carried
            x = mean_step(t, x, y)
            obs, r_row = step_rows(t)
            y = obs - x[:, :gauges]
            a = pred_ref[...]
            slot = jnp.where(t == me, 0, 1)
            kept_ref[slot] = a
            kept_rows_ref[slot] = jnp.broadcast_to(
                jnp.concatenate([x, y], axis=1), (8, states + gauges)
            )
            s = a[:gauges, :gauges] + eye * r_row
            d_row = 1.0 / jnp.sum(eye * s, axis=0, keepdims=True)
            d_col = 1.0 / jnp.sum(eye * s, axis=1, keepdims=True)
            a_s = split(a)
            fs = (f_ref[0], f_ref[1])
            aft = dot3(a_s, (ft_ref[0], ft_ref[1]))
            nxt = dot3(fs, split(aft)) + q_ref[...]
            ct = aft[:gauges]
            if robust:
                root_row, root_col = jnp.sqrt(d_row), jnp.sqrt(d_col)
                w = gauss_jordan(s * root_col * root_row) * root_col * root_row
                wct = full(w, ct)
                pred_ref[...] = nxt - full(ct.T, wct)
                gain_ref[t + 1] = jnp.concatenate([w, wct], axis=1)
                return x, y
            e = eye - s * d_row
            es = split(e)
            u = dot3(es, es)
            c = dot3(fs, (a_s[0][:, :gauges], a_s[1][:, :gauges]))
            us = split(u)
            ed = e * d_col
            ud = u * d_col
            ct_s = split(ct)
            c_s = split(c)
            right = [ct, dot3(es, ct_s), dot3(us, ct_s)]
            left_both = dot3(c_s, split(jnp.concatenate([ed, ud], axis=1)))
            left = [c * d_row, left_both[:, :gauges], left_both[:, gauges:]]
            powers = [eye, e, u]
            if HALF_DEGREE == 4:
                ub = us[0]
                more = dot(
                    ub,
                    jnp.concatenate(
                        [right[1].astype(BF16), right[2].astype(BF16), es[0], ub], axis=1
                    ),
                )
                right += [more[:, :states], more[:, states : 2 * states]]
                powers += [
                    more[:, 2 * states : 2 * states + gauges],
                    more[:, 2 * states + gauges :],
                ]
                lb = dot(
                    jnp.concatenate(
                        [left[1].astype(BF16), left[2].astype(BF16)], axis=0
                    ),
                    ub,
                )
                left += [lb[:states], lb[states:]]
            mix = lambda cs, ms: sum(c * m for c, m in zip(cs[1:], ms[1:])) + cs[0] * ms[0]
            rt = split(mix(second, right))
            pred_ref[...] = nxt - dot3(split(mix(first, left)), rt)
            bs = split(mix(second, powers))
            poly = dot3(
                split(mix(first, powers)),
                (
                    jnp.concatenate([bs[0], rt[0]], axis=1),
                    jnp.concatenate([bs[1], rt[1]], axis=1),
                ),
            )
            poly_ref[t] = jnp.concatenate([e, poly[:, :gauges]], axis=1)
            gain_ref[t + 1] = poly * d_col
            return x, y

        zero = jnp.zeros((1, states), F32)
        x, y = lax.fori_loop(0, steps, forward, (zero, jnp.zeros((1, gauges), F32)))
        mean_step(steps, x, y)

        def backward(i, carried):
            lam, worst = carried
            t = steps - 1 - i
            slot = jnp.where(t == me, 2, 3)
            hat = jnp.broadcast_to(lam, (16, states))
            hs = split(hat)
            hat = dot3(hs, (f_ref[0], f_ref[1]))[:1]
            kept_rows_ref[slot] = jnp.broadcast_to(
                jnp.concatenate([hat, rows_ref[t + 1]], axis=1), (8, states + gauges)
            )
            gain = gain_ref[t + 1]
            kept_gain_ref[jnp.where(t == me, 0, 1)] = gain[:, :gauges]
            fix = dot3_t(hs, split(gain[:, gauges:]))[:1]
            if not robust:
                both = poly_ref[t]
                e, poly = both[:, :gauges], both[:, gauges:]
                residual = eye - poly + dot3(split(e), split(poly))
                worst = jnp.maximum(
                    worst, jnp.sum(residual * residual, axis=0, keepdims=True)
                )
            new = jnp.concatenate(
                [hat[:, :gauges] - rows_ref[t + 1] - fix, hat[:, gauges:]], axis=1
            )
            return new, worst

        nothing, worst = lax.fori_loop(
            0, steps, backward, (zero, jnp.zeros((1, gauges), F32))
        )
        return jnp.sum(worst)

    worst = run(False)

    @pl.when(jnp.logical_not(worst < RESIDUAL_LIMIT))
    def _():
        run(True)

    perm = perm_ref[...]
    a = kept_ref[0]
    w = kept_gain_ref[0]
    a_o = a[:gauges]
    r_row = step_rows(me)[1]
    s = a_o[:, :gauges] + eye * r_row
    ws = split(w)
    residual = eye - dot3(ws, split(s))
    w = w + dot(residual.astype(BF16), ws[0])
    k = dot3(split(w), split(a_o))
    cov = a - dot3(split(a[:, :gauges]), split(k))
    cov_ref[0] = move(perm_t_ref[...], move(cov, perm))
    rows, lam = kept_rows_ref[0], kept_rows_ref[2][:, :states]
    x, y = rows[:, :states], rows[:, states:]
    mean = x + dot3(split(y), split(k))
    smooth = mean - dot3(split(lam), split(cov))
    filtered_ref[...] = move(mean, perm)[:1]
    smoothed_ref[...] = move(smooth, perm)[:1]


def shards(observations, noise_var, gauge_index, dynamics, process):
    states = dynamics.shape[0]
    gauges = gauge_index.shape[0]
    steps = lax.axis_size("tm")
    vmem = pl.BlockSpec(memory_space=pltpu.VMEM)
    gathered = pl.pallas_call(
        functools.partial(gather_kernel, steps),
        out_shape=jax.ShapeDtypeStruct((steps, 1, 2 * gauges), F32),
        in_specs=[vmem] * 2,
        out_specs=vmem,
        scratch_shapes=[
            pltpu.VMEM((1, 1, 2 * gauges), F32),
            pltpu.SemaphoreType.DMA((steps,)),
            pltpu.SemaphoreType.DMA((steps,)),
        ],
        compiler_params=pltpu.CompilerParams(collective_id=0, has_side_effects=True),
    )(observations, noise_var)
    return pl.pallas_call(
        functools.partial(kernel, steps),
        out_shape=(
            jax.ShapeDtypeStruct((1, states), F32),
            jax.ShapeDtypeStruct((1, states, states), F32),
            jax.ShapeDtypeStruct((1, states), F32),
        ),
        in_specs=[vmem] * 4,
        out_specs=(vmem,) * 3,
        scratch_shapes=[
            pltpu.VMEM((2, states, states), BF16),
            pltpu.VMEM((2, states, states), BF16),
            pltpu.VMEM((states, states), F32),
            pltpu.VMEM((states, states), BF16),
            pltpu.VMEM((states, states), BF16),
            pltpu.VMEM((states, states), F32),
            pltpu.VMEM((steps + 1, gauges, gauges + states), F32),
            pltpu.VMEM((steps, gauges, 2 * gauges), F32),
            pltpu.VMEM((steps + 1, 1, gauges), F32),
            pltpu.VMEM((2, states, states), F32),
            pltpu.VMEM((2, gauges, gauges), F32),
            pltpu.VMEM((4, 8, states + gauges), F32),
            pltpu.VMEM((gauges, gauges), F32),
        ],
        compiler_params=pltpu.CompilerParams(vmem_limit_bytes=56 * 1024 * 1024),
    )(gathered, gauge_index.reshape(1, gauges), dynamics, process)


def solution(mesh):
    return jax.shard_map(
        shards,
        mesh=mesh,
        in_specs=(P(("groups", "tm"), None), P(("groups", "tm"), None), P("groups"), P(), P()),
        out_specs=(
            P(("groups", "tm"), None),
            P(("groups", "tm"), None, None),
            P(("groups", "tm"), None),
        ),
        check_vma=False,
    )
```

```python
import functools

import jax
import jax.numpy as jnp
import numpy as np
from jax import lax
from jax.experimental import pallas as pl
from jax.experimental.pallas import tpu as pltpu
from jax.sharding import PartitionSpec as P

F32 = jnp.float32
BF16 = jnp.bfloat16
HIGHEST = lax.Precision.HIGHEST
MESH = pl.DeviceIdType.MESH
RADIUS = 0.3
HALF_DEGREE = 2
RESIDUAL_LIMIT = 4e-6


def split(a):
    high = a.astype(BF16)
    return high, (a - high.astype(F32)).astype(BF16)


def dot(a, b):
    return jnp.dot(a, b, preferred_element_type=F32)


def dot3(a, b):
    (ah, al), (bh, bl) = a, b
    return dot(
        jnp.concatenate([ah, ah, al], axis=1), jnp.concatenate([bh, bl, bh], axis=0)
    )


def dot_t(a, b):
    return lax.dot_general(a, b, (((1,), (1,)), ((), ())), preferred_element_type=F32)


def full(a, b):
    return jnp.dot(a, b, precision=HIGHEST, preferred_element_type=F32)


def iotas(shape):
    return (
        lax.broadcasted_iota(jnp.int32, shape, 0),
        lax.broadcasted_iota(jnp.int32, shape, 1),
    )


def permutation(index_row, states, gauges):
    rows, cols = iotas((states, gauges))
    gauged = (rows == index_row).astype(F32)
    free = 1.0 - jnp.sum(gauged, axis=1, keepdims=True)
    r, c = iotas((states, states))
    below = (c < r).astype(F32)
    rank = dot(below, jnp.broadcast_to(free, (states, gauges)))
    others = jnp.where(rank == cols.astype(F32), free, 0.0)
    return jnp.concatenate([gauged, others], axis=1)


def dot3_t(a, b):
    (ah, al), (bh, bl) = a, b
    return dot_t(jnp.concatenate([ah, ah, al], axis=1), jnp.concatenate([bh, bl, bh], axis=1))


def move(a, b):
    if a.dtype == BF16:
        high, low = split(b)
        return dot(a, high) + dot(a, low)
    high, low = split(a)
    return dot(high, b) + dot(low, b)


def factors():
    degree = 2 * HALF_DEGREE
    z = 1.0 / RADIUS
    u = [np.poly1d([1.0]), np.poly1d([2.0, 0.0])]
    for _ in range(degree):
        u.append(np.poly1d([2.0, 0.0]) * u[-1] - u[-2])
    rest = sum((k(z) * k for k in u), np.poly1d([0.0])) / sum(k(z) ** 2 for k in u)
    scaled = np.poly1d([c * z ** (len(rest.coeffs) - 1 - i) for i, c in enumerate(rest.coeffs)])
    quotient, _ = np.polydiv((np.poly1d([1.0]) - scaled).coeffs, np.array([-1.0, 1.0]))
    roots = sorted(np.roots(quotient), key=lambda r: (abs(r.imag) < 1e-9, r.real, r.imag))
    pick = [r for i, r in enumerate(roots) if (i // 2) % 2 == 0]
    other = [r for i, r in enumerate(roots) if (i // 2) % 2 == 1]
    first = np.real(np.poly(pick))
    first = first / first[-1]
    second = np.real(np.poly(other))
    second = second / second[-1] * quotient[-1]
    return [float(c) for c in first[::-1]], [float(c) for c in second[::-1]]


def gather_kernel(
    count,
    obs_ref,
    var_ref,
    index_ref,
    dynamics_ref,
    process_ref,
    out_ref,
    f_ref,
    ft_ref,
    q_ref,
    perm_ref,
    perm_t_ref,
    row_ref,
    send_sem,
    recv_sem,
):
    me = lax.axis_index("tm")
    group = lax.axis_index("groups")
    gauges = obs_ref.shape[1]
    barrier = pltpu.get_barrier_semaphore()

    def greet(d, nothing):
        peer = lax.rem(me + d, count)
        pl.semaphore_signal(barrier, inc=1, device_id=(group, peer), device_id_type=MESH)
        return nothing

    lax.fori_loop(1, count, greet, 0)
    row_ref[0, :, :gauges] = obs_ref[...]
    row_ref[0, :, gauges:] = var_ref[...]
    out_ref[me] = row_ref[0]
    states = dynamics_ref.shape[0]
    perm_t = permutation(index_ref[...], states, gauges)
    perm = perm_t.T.astype(BF16)
    perm_t = perm_t.astype(BF16)
    perm_ref[...] = perm
    perm_t_ref[...] = perm_t
    pl.semaphore_wait(barrier, count - 1)

    def copy(d):
        peer = lax.rem(me + d, count)
        return pltpu.make_async_remote_copy(
            src_ref=row_ref.at[0],
            dst_ref=out_ref.at[me],
            send_sem=send_sem.at[d],
            recv_sem=recv_sem.at[d],
            device_id=(group, peer),
            device_id_type=MESH,
        )

    def start(d, nothing):
        copy(d).start()
        return nothing

    def finish(d, nothing):
        copy(d).wait()
        return nothing

    lax.fori_loop(1, count, start, 0)
    f = move(move(perm, dynamics_ref[...]), perm_t)
    f_ref[0], f_ref[1] = split(f)
    ft_ref[0], ft_ref[1] = split(f.T)
    q_ref[...] = move(move(perm, process_ref[...]), perm_t)
    lax.fori_loop(1, count, finish, 0)


def kernel(
    steps,
    gathered_ref,
    f_ref,
    ft_ref,
    q_ref,
    perm_ref,
    perm_t_ref,
    filtered_ref,
    cov_ref,
    smoothed_ref,
    pred_ref,
    gain_ref,
    poly_ref,
    rows_ref,
    kept_ref,
    kept_gain_ref,
    kept_rows_ref,
    work_ref,
):
    states = q_ref.shape[0]
    gauges = gathered_ref.shape[2] // 2
    me = lax.axis_index("tm")
    rg, cg = iotas((gauges, gauges))
    eye = (rg == cg).astype(F32)
    first, second = factors()

    def gauss_jordan(s):
        work_ref[...] = s

        def pivot(k, nothing):
            m = work_ref[...]
            row = jnp.sum(jnp.where(rg == k, m, 0.0), axis=0, keepdims=True)
            col = jnp.sum(jnp.where(cg == k, m, 0.0), axis=1, keepdims=True)
            inv = 1.0 / jnp.sum(jnp.where(cg[:1] == k, row, 0.0), axis=1, keepdims=True)
            scaled = row * inv
            new = m - col * scaled
            new = jnp.where(cg == k, -col * inv, new)
            new_row = jnp.where(cg[:1] == k, inv, scaled)
            work_ref[...] = jnp.where(rg == k, new_row, new)
            return nothing

        lax.fori_loop(0, gauges, pivot, 0)
        return work_ref[...]

    def mix(coefficients, terms):
        return sum(c * m for c, m in zip(coefficients[1:], terms[1:])) + coefficients[0] * terms[0]

    def step_rows(t):
        row = gathered_ref[t]
        return row[:, :gauges], row[:, gauges:]

    def run(robust):
        pred_ref[...] = q_ref[...]
        gain_ref[0] = jnp.zeros_like(gain_ref[0])

        def gained(t, y):
            gy = dot3_t(split(jnp.broadcast_to(y, (16, gauges))), split(gain_ref[t]))[:1]
            rows_ref[t] = gy[:, :gauges]
            return gy[:, gauges:]

        def forward(t, carried):
            x, y = carried
            obs, r_row = step_rows(t)
            a = pred_ref[...]
            s = a[:gauges, :gauges] + eye * r_row
            d_row = 1.0 / jnp.sum(eye * s, axis=0, keepdims=True)
            d_col = 1.0 / jnp.sum(eye * s, axis=1, keepdims=True)
            fs = (f_ref[0], f_ref[1])
            tall = jnp.concatenate([a, jnp.broadcast_to(x, (16, states))], axis=0)
            aft = dot3(split(tall), (ft_ref[0], ft_ref[1]))
            ct = aft[:gauges]
            if not robust:
                e = eye - s * d_row
                es = split(e)
                u = dot3(es, es)
                us = split(u)
                stacked = (
                    jnp.concatenate([es[0], us[0]], axis=0),
                    jnp.concatenate([es[1], us[1]], axis=0),
                )
                eu = dot3(stacked, split(ct))
                right = [ct, eu[:gauges], eu[gauges:]]
                powers = [eye, e, u]
                left = (mix(first, right) * d_col).T
                ls, rs = split(left), split(mix(second, right))
                prod = dot3(ls, rs)
            nxt = dot3(fs, split(aft[:states])) + q_ref[...]
            x = aft[states : states + 1] + gained(t, y)
            y = obs - x[:, :gauges]
            slot = jnp.where(t == me, 0, 1)
            kept_ref[slot] = a
            kept_rows_ref[slot] = jnp.broadcast_to(
                jnp.concatenate([x, y], axis=1), (8, states + gauges)
            )
            if robust:
                root_row, root_col = jnp.sqrt(d_row), jnp.sqrt(d_col)
                w = gauss_jordan(s * root_col * root_row) * root_col * root_row
                wct = full(w, ct)
                pred_ref[...] = nxt - full(ct.T, wct)
                gain_ref[t + 1] = jnp.concatenate([w, wct.T], axis=0)
                return x, y
            pred_ref[...] = nxt - prod
            ps = split(mix(first, powers) * d_col)
            gain = dot3(
                (
                    jnp.concatenate([ps[0], ls[0]], axis=0),
                    jnp.concatenate([ps[1], ls[1]], axis=0),
                ),
                split(mix(second, powers)),
            )
            gain_ref[t + 1] = gain
            poly_ref[t] = s
            return x, y

        zero = jnp.zeros((1, states), F32)
        x, y = lax.fori_loop(0, steps, forward, (zero, jnp.zeros((1, gauges), F32)), unroll=4)
        gained(steps, y)

        def backward(i, carried):
            lam, worst = carried
            t = steps - 1 - i
            slot = jnp.where(t == me, 2, 3)
            hat = jnp.broadcast_to(lam, (16, states))
            hs = split(hat)
            hat = dot3(hs, (f_ref[0], f_ref[1]))[:1]
            kept_rows_ref[slot] = jnp.broadcast_to(
                jnp.concatenate([hat, rows_ref[t + 1]], axis=1), (8, states + gauges)
            )
            gain = gain_ref[t + 1]
            kept_gain_ref[jnp.where(t == me, 0, 1)] = gain[:gauges]
            fix = dot3(hs, split(gain[gauges:]))[:1]
            if not robust:
                residual = eye - dot3(split(poly_ref[t]), split(gain[:gauges]))
                worst = jnp.maximum(
                    worst, jnp.sum(residual * residual, axis=0, keepdims=True)
                )
            new = jnp.concatenate(
                [hat[:, :gauges] - rows_ref[t + 1] - fix, hat[:, gauges:]], axis=1
            )
            return new, worst

        nothing, worst = lax.fori_loop(
            0, steps, backward, (zero, jnp.zeros((1, gauges), F32))
        )
        return jnp.sum(worst)

    worst = run(False)

    @pl.when(jnp.logical_not(worst < RESIDUAL_LIMIT))
    def _():
        run(True)

    perm = perm_ref[...]
    a = kept_ref[0]
    w = kept_gain_ref[0]
    a_o = a[:gauges]
    r_row = step_rows(me)[1]
    s = a_o[:, :gauges] + eye * r_row
    ws = split(w)
    residual = eye - dot3(ws, split(s))
    w = w + dot(residual.astype(BF16), ws[0])
    k = dot3(split(w), split(a_o))
    cov = a - dot3(split(a[:, :gauges]), split(k))
    cov_ref[0] = move(perm_t_ref[...], move(cov, perm))
    rows, lam = kept_rows_ref[0], kept_rows_ref[2][:, :states]
    x, y = rows[:, :states], rows[:, states:]
    mean = x + dot3(split(y), split(k))
    smooth = mean - dot3(split(lam), split(cov))
    filtered_ref[...] = move(mean, perm)[:1]
    smoothed_ref[...] = move(smooth, perm)[:1]


def shards(observations, noise_var, gauge_index, dynamics, process):
    states = dynamics.shape[0]
    gauges = gauge_index.shape[0]
    steps = lax.axis_size("tm")
    vmem = pl.BlockSpec(memory_space=pltpu.VMEM)
    square = jax.ShapeDtypeStruct((states, states), BF16)
    pair = jax.ShapeDtypeStruct((2, states, states), BF16)
    prepared = pl.pallas_call(
        functools.partial(gather_kernel, steps),
        out_shape=(
            jax.ShapeDtypeStruct((steps, 1, 2 * gauges), F32),
            pair,
            pair,
            jax.ShapeDtypeStruct((states, states), F32),
            square,
            square,
        ),
        in_specs=[vmem] * 5,
        out_specs=(vmem,) * 6,
        scratch_shapes=[
            pltpu.VMEM((1, 1, 2 * gauges), F32),
            pltpu.SemaphoreType.DMA((steps,)),
            pltpu.SemaphoreType.DMA((steps,)),
        ],
        compiler_params=pltpu.CompilerParams(collective_id=0, has_side_effects=True, vmem_limit_bytes=56 * 1024 * 1024),
    )(observations, noise_var, gauge_index.reshape(1, gauges), dynamics, process)
    return pl.pallas_call(
        functools.partial(kernel, steps),
        out_shape=(
            jax.ShapeDtypeStruct((1, states), F32),
            jax.ShapeDtypeStruct((1, states, states), F32),
            jax.ShapeDtypeStruct((1, states), F32),
        ),
        in_specs=[vmem] * 6,
        out_specs=(vmem,) * 3,
        scratch_shapes=[
            pltpu.VMEM((states, states), F32),
            pltpu.VMEM((steps + 1, gauges + states, gauges), F32),
            pltpu.VMEM((steps, gauges, gauges), F32),
            pltpu.VMEM((steps + 1, 1, gauges), F32),
            pltpu.VMEM((2, states, states), F32),
            pltpu.VMEM((2, gauges, gauges), F32),
            pltpu.VMEM((4, 8, states + gauges), F32),
            pltpu.VMEM((gauges, gauges), F32),
        ],
        compiler_params=pltpu.CompilerParams(vmem_limit_bytes=56 * 1024 * 1024),
    )(*prepared)


def solution(mesh):
    return jax.shard_map(
        shards,
        mesh=mesh,
        in_specs=(P(("groups", "tm"), None), P(("groups", "tm"), None), P("groups"), P(), P()),
        out_specs=(
            P(("groups", "tm"), None),
            P(("groups", "tm"), None, None),
            P(("groups", "tm"), None),
        ),
        check_vma=False,
    )
```

```python
import functools

import jax
import jax.numpy as jnp
import numpy as np
from jax import lax
from jax.experimental import pallas as pl
from jax.experimental.pallas import tpu as pltpu
from jax.sharding import PartitionSpec as P

F32 = jnp.float32
BF16 = jnp.bfloat16
HIGHEST = lax.Precision.HIGHEST
MESH = pl.DeviceIdType.MESH
RADIUS = 0.27
HALF_DEGREE = 2
RESIDUAL_LIMIT = 4e-6


def split(a):
    high = a.astype(BF16)
    return high, (a - high.astype(F32)).astype(BF16)


def dot(a, b):
    return jnp.dot(a, b, preferred_element_type=F32)


def dot3(a, b):
    (ah, al), (bh, bl) = a, b
    return dot(
        jnp.concatenate([ah, ah, al], axis=1), jnp.concatenate([bh, bl, bh], axis=0)
    )


def dot_t(a, b):
    return lax.dot_general(a, b, (((1,), (1,)), ((), ())), preferred_element_type=F32)


def full(a, b):
    return jnp.dot(a, b, precision=HIGHEST, preferred_element_type=F32)


def iotas(shape):
    return (
        lax.broadcasted_iota(jnp.int32, shape, 0),
        lax.broadcasted_iota(jnp.int32, shape, 1),
    )


def permutation(index_row, states, gauges):
    rows, cols = iotas((states, gauges))
    gauged = (rows == index_row).astype(F32)
    free = 1.0 - jnp.sum(gauged, axis=1, keepdims=True)
    r, c = iotas((states, states))
    below = (c < r).astype(F32)
    rank = dot(below, jnp.broadcast_to(free, (states, gauges)))
    others = jnp.where(rank == cols.astype(F32), free, 0.0)
    return jnp.concatenate([gauged, others], axis=1)


def dot3_t(a, b):
    (ah, al), (bh, bl) = a, b
    return dot_t(jnp.concatenate([ah, ah, al], axis=1), jnp.concatenate([bh, bl, bh], axis=1))


def move(a, b):
    if a.dtype == BF16:
        high, low = split(b)
        return dot(a, high) + dot(a, low)
    high, low = split(a)
    return dot(high, b) + dot(low, b)


def factors():
    degree = 2 * HALF_DEGREE
    z = 1.0 / RADIUS
    u = [np.poly1d([1.0]), np.poly1d([2.0, 0.0])]
    for _ in range(degree):
        u.append(np.poly1d([2.0, 0.0]) * u[-1] - u[-2])
    rest = sum((k(z) * k for k in u), np.poly1d([0.0])) / sum(k(z) ** 2 for k in u)
    scaled = np.poly1d([c * z ** (len(rest.coeffs) - 1 - i) for i, c in enumerate(rest.coeffs)])
    quotient, _ = np.polydiv((np.poly1d([1.0]) - scaled).coeffs, np.array([-1.0, 1.0]))
    roots = sorted(np.roots(quotient), key=lambda r: (abs(r.imag) < 1e-9, r.real, r.imag))
    pick = [r for i, r in enumerate(roots) if (i // 2) % 2 == 0]
    other = [r for i, r in enumerate(roots) if (i // 2) % 2 == 1]
    first = np.real(np.poly(pick))
    first = first / first[-1]
    second = np.real(np.poly(other))
    second = second / second[-1] * quotient[-1]
    return [float(c) for c in first[::-1]], [float(c) for c in second[::-1]]


def gather_kernel(
    count,
    obs_ref,
    var_ref,
    index_ref,
    dynamics_hbm,
    process_hbm,
    out_ref,
    f_ref,
    ft_ref,
    q_ref,
    perm_ref,
    perm_t_ref,
    row_ref,
    dynamics_ref,
    process_ref,
    load_sem,
    send_sem,
    recv_sem,
):
    me = lax.axis_index("tm")
    group = lax.axis_index("groups")
    gauges = obs_ref.shape[1]
    barrier = pltpu.get_barrier_semaphore()

    def greet(d, nothing):
        peer = lax.rem(me + d, count)
        pl.semaphore_signal(barrier, inc=1, device_id=(group, peer), device_id_type=MESH)
        return nothing

    lax.fori_loop(1, count, greet, 0)
    loads = [
        pltpu.make_async_copy(dynamics_hbm, dynamics_ref, load_sem.at[0]),
        pltpu.make_async_copy(process_hbm, process_ref, load_sem.at[1]),
    ]
    for load in loads:
        load.start()
    row_ref[0, :, :gauges] = obs_ref[...]
    row_ref[0, :, gauges:] = var_ref[...]
    out_ref[me] = row_ref[0]
    states = dynamics_ref.shape[0]
    perm_t = permutation(index_ref[...], states, gauges)
    perm = perm_t.T.astype(BF16)
    perm_t = perm_t.astype(BF16)
    perm_ref[...] = perm
    perm_t_ref[...] = perm_t
    pl.semaphore_wait(barrier, count - 1)

    def copy(d):
        peer = lax.rem(me + d, count)
        return pltpu.make_async_remote_copy(
            src_ref=row_ref.at[0],
            dst_ref=out_ref.at[me],
            send_sem=send_sem.at[d],
            recv_sem=recv_sem.at[d],
            device_id=(group, peer),
            device_id_type=MESH,
        )

    def start(d, nothing):
        copy(d).start()
        return nothing

    def finish(d, nothing):
        copy(d).wait()
        return nothing

    lax.fori_loop(1, count, start, 0)
    for load in loads:
        load.wait()
    f = move(move(perm, dynamics_ref[...]), perm_t)
    f_ref[0], f_ref[1] = split(f)
    ft_ref[0], ft_ref[1] = split(f.T)
    q_ref[...] = move(move(perm, process_ref[...]), perm_t)
    lax.fori_loop(1, count, finish, 0)


def kernel(
    steps,
    gathered_ref,
    f_ref,
    ft_ref,
    q_ref,
    perm_ref,
    perm_t_ref,
    filtered_ref,
    cov_ref,
    smoothed_ref,
    pred_ref,
    gain_ref,
    poly_ref,
    rows_ref,
    kept_ref,
    kept_gain_ref,
    kept_rows_ref,
    work_ref,
):
    states = q_ref.shape[0]
    gauges = gathered_ref.shape[2] // 2
    me = lax.axis_index("tm")
    rg, cg = iotas((gauges, gauges))
    eye = (rg == cg).astype(F32)
    first, second = factors()

    def gauss_jordan(s):
        work_ref[...] = s

        def pivot(k, nothing):
            m = work_ref[...]
            row = jnp.sum(jnp.where(rg == k, m, 0.0), axis=0, keepdims=True)
            col = jnp.sum(jnp.where(cg == k, m, 0.0), axis=1, keepdims=True)
            inv = 1.0 / jnp.sum(jnp.where(cg[:1] == k, row, 0.0), axis=1, keepdims=True)
            scaled = row * inv
            new = m - col * scaled
            new = jnp.where(cg == k, -col * inv, new)
            new_row = jnp.where(cg[:1] == k, inv, scaled)
            work_ref[...] = jnp.where(rg == k, new_row, new)
            return nothing

        lax.fori_loop(0, gauges, pivot, 0)
        return work_ref[...]

    def mix(coefficients, terms):
        return sum(c * m for c, m in zip(coefficients[1:], terms[1:])) + coefficients[0] * terms[0]

    def step_rows(t):
        row = gathered_ref[t]
        return row[:, :gauges], row[:, gauges:]

    def run(robust):
        pred_ref[...] = q_ref[...]
        gain_ref[0] = jnp.zeros_like(gain_ref[0])

        def gained(t, y):
            gy = dot3_t(split(jnp.broadcast_to(y, (16, gauges))), split(gain_ref[t]))[:1]
            rows_ref[t] = gy[:, :gauges]
            return gy[:, gauges:]

        def forward(t, carried):
            x, y = carried
            obs, r_row = step_rows(t)
            a = pred_ref[...]
            s = a[:gauges, :gauges] + eye * r_row
            d_row = 1.0 / jnp.sum(eye * s, axis=0, keepdims=True)
            d_col = 1.0 / jnp.sum(eye * s, axis=1, keepdims=True)
            fs = (f_ref[0], f_ref[1])
            tall = jnp.concatenate([a, jnp.broadcast_to(x, (16, states))], axis=0)
            aft = dot3(split(tall), (ft_ref[0], ft_ref[1]))
            ct = aft[:gauges]
            if not robust:
                e = eye - s * d_row
                es = split(e)
                u = dot3(es, es)
                us = split(u)
                stacked = (
                    jnp.concatenate([es[0], us[0]], axis=0),
                    jnp.concatenate([es[1], us[1]], axis=0),
                )
                eu = dot3(stacked, split(ct))
                right = [ct, eu[:gauges], eu[gauges:]]
                powers = [eye, e, u]
                left = (mix(first, right) * d_col).T
                ls, rs = split(left), split(mix(second, right))
                prod = dot3(ls, rs)
            nxt = dot3(fs, split(aft[:states])) + q_ref[...]
            x = aft[states : states + 1] + gained(t, y)
            y = obs - x[:, :gauges]
            slot = jnp.where(t == me, 0, 1)
            kept_ref[slot] = a
            kept_rows_ref[slot] = jnp.broadcast_to(
                jnp.concatenate([x, y], axis=1), (8, states + gauges)
            )
            if robust:
                root_row, root_col = jnp.sqrt(d_row), jnp.sqrt(d_col)
                w = gauss_jordan(s * root_col * root_row) * root_col * root_row
                wct = full(w, ct)
                pred_ref[...] = nxt - full(ct.T, wct)
                gain_ref[t + 1] = jnp.concatenate([w, wct.T], axis=0)
                return x, y
            pred_ref[...] = nxt - prod
            ps = split(mix(first, powers) * d_col)
            gain = dot3(
                (
                    jnp.concatenate([ps[0], ls[0]], axis=0),
                    jnp.concatenate([ps[1], ls[1]], axis=0),
                ),
                split(mix(second, powers)),
            )
            gain_ref[t + 1] = gain
            poly_ref[t] = s
            return x, y

        zero = jnp.zeros((1, states), F32)
        x, y = lax.fori_loop(0, steps, forward, (zero, jnp.zeros((1, gauges), F32)), unroll=4)
        gained(steps, y)

        def backward(i, carried):
            lam, worst = carried
            t = steps - 1 - i
            slot = jnp.where(t == me, 2, 3)
            hat = jnp.broadcast_to(lam, (16, states))
            hs = split(hat)
            hat = dot3(hs, (f_ref[0], f_ref[1]))[:1]
            kept_rows_ref[slot] = jnp.broadcast_to(
                jnp.concatenate([hat, rows_ref[t + 1]], axis=1), (8, states + gauges)
            )
            gain = gain_ref[t + 1]
            kept_gain_ref[jnp.where(t == me, 0, 1)] = gain[:gauges]
            fix = dot3(hs, split(gain[gauges:]))[:1]
            if not robust:
                residual = eye - dot3(split(poly_ref[t]), split(gain[:gauges]))
                worst = jnp.maximum(
                    worst, jnp.sum(residual * residual, axis=0, keepdims=True)
                )
            new = jnp.concatenate(
                [hat[:, :gauges] - rows_ref[t + 1] - fix, hat[:, gauges:]], axis=1
            )
            return new, worst

        nothing, worst = lax.fori_loop(
            0, steps, backward, (zero, jnp.zeros((1, gauges), F32)), unroll=4
        )
        return jnp.sum(worst)

    worst = run(False)

    @pl.when(jnp.logical_not(worst < RESIDUAL_LIMIT))
    def _():
        run(True)

    perm = perm_ref[...]
    a = kept_ref[0]
    w = kept_gain_ref[0]
    a_o = a[:gauges]
    r_row = step_rows(me)[1]
    s = a_o[:, :gauges] + eye * r_row
    ws = split(w)
    residual = eye - dot3(ws, split(s))
    w = w + dot(residual.astype(BF16), ws[0])
    k = dot3(split(w), split(a_o))
    cov = a - dot3(split(a[:, :gauges]), split(k))
    cov_ref[0] = move(perm_t_ref[...], move(cov, perm))
    rows, lam = kept_rows_ref[0], kept_rows_ref[2][:, :states]
    x, y = rows[:, :states], rows[:, states:]
    mean = x + dot3(split(y), split(k))
    smooth = mean - dot3(split(lam), split(cov))
    filtered_ref[...] = move(mean, perm)[:1]
    smoothed_ref[...] = move(smooth, perm)[:1]


def shards(observations, noise_var, gauge_index, dynamics, process):
    states = dynamics.shape[0]
    gauges = gauge_index.shape[0]
    steps = lax.axis_size("tm")
    vmem = pl.BlockSpec(memory_space=pltpu.VMEM)
    square = jax.ShapeDtypeStruct((states, states), BF16)
    pair = jax.ShapeDtypeStruct((2, states, states), BF16)
    prepared = pl.pallas_call(
        functools.partial(gather_kernel, steps),
        out_shape=(
            jax.ShapeDtypeStruct((steps, 1, 2 * gauges), F32),
            pair,
            pair,
            jax.ShapeDtypeStruct((states, states), F32),
            square,
            square,
        ),
        in_specs=[vmem] * 3 + [pl.BlockSpec(memory_space=pl.ANY)] * 2,
        out_specs=(vmem,) * 6,
        scratch_shapes=[
            pltpu.VMEM((1, 1, 2 * gauges), F32),
            pltpu.VMEM((states, states), F32),
            pltpu.VMEM((states, states), F32),
            pltpu.SemaphoreType.DMA((2,)),
            pltpu.SemaphoreType.DMA((steps,)),
            pltpu.SemaphoreType.DMA((steps,)),
        ],
        compiler_params=pltpu.CompilerParams(collective_id=0, has_side_effects=True, vmem_limit_bytes=56 * 1024 * 1024),
    )(observations, noise_var, gauge_index.reshape(1, gauges), dynamics, process)
    return pl.pallas_call(
        functools.partial(kernel, steps),
        out_shape=(
            jax.ShapeDtypeStruct((1, states), F32),
            jax.ShapeDtypeStruct((1, states, states), F32),
            jax.ShapeDtypeStruct((1, states), F32),
        ),
        in_specs=[vmem] * 6,
        out_specs=(vmem,) * 3,
        scratch_shapes=[
            pltpu.VMEM((states, states), F32),
            pltpu.VMEM((steps + 1, gauges + states, gauges), F32),
            pltpu.VMEM((steps, gauges, gauges), F32),
            pltpu.VMEM((steps + 1, 1, gauges), F32),
            pltpu.VMEM((2, states, states), F32),
            pltpu.VMEM((2, gauges, gauges), F32),
            pltpu.VMEM((4, 8, states + gauges), F32),
            pltpu.VMEM((gauges, gauges), F32),
        ],
        compiler_params=pltpu.CompilerParams(vmem_limit_bytes=56 * 1024 * 1024),
    )(*prepared)


def solution(mesh):
    return jax.shard_map(
        shards,
        mesh=mesh,
        in_specs=(P(("groups", "tm"), None), P(("groups", "tm"), None), P("groups"), P(), P()),
        out_specs=(
            P(("groups", "tm"), None),
            P(("groups", "tm"), None, None),
            P(("groups", "tm"), None),
        ),
        check_vma=False,
    )
```

```python
import functools

import jax
import jax.numpy as jnp
import numpy as np
from jax import lax
from jax.experimental import pallas as pl
from jax.experimental.pallas import tpu as pltpu
from jax.sharding import PartitionSpec as P

F32 = jnp.float32
BF16 = jnp.bfloat16
HIGHEST = lax.Precision.HIGHEST
MESH = pl.DeviceIdType.MESH
RADIUS = 0.27
HALF_DEGREE = 2
RESIDUAL_LIMIT = 4e-6


def split(a):
    high = a.astype(BF16)
    return high, (a - high.astype(F32)).astype(BF16)


def dot(a, b):
    return jnp.dot(a, b, preferred_element_type=F32)


def dot3(a, b):
    (ah, al), (bh, bl) = a, b
    return dot(
        jnp.concatenate([ah, ah, al], axis=1), jnp.concatenate([bh, bl, bh], axis=0)
    )


def dot_t(a, b):
    return lax.dot_general(a, b, (((1,), (1,)), ((), ())), preferred_element_type=F32)


def full(a, b):
    return jnp.dot(a, b, precision=HIGHEST, preferred_element_type=F32)


def iotas(shape):
    return (
        lax.broadcasted_iota(jnp.int32, shape, 0),
        lax.broadcasted_iota(jnp.int32, shape, 1),
    )


def permutation(index_row, states, gauges):
    rows, cols = iotas((states, gauges))
    gauged = (rows == index_row).astype(F32)
    free = 1.0 - jnp.sum(gauged, axis=1, keepdims=True)
    r, c = iotas((states, states))
    below = (c < r).astype(F32)
    rank = dot(below, jnp.broadcast_to(free, (states, gauges)))
    others = jnp.where(rank == cols.astype(F32), free, 0.0)
    return jnp.concatenate([gauged, others], axis=1)


def dot3_t(a, b):
    (ah, al), (bh, bl) = a, b
    return dot_t(jnp.concatenate([ah, ah, al], axis=1), jnp.concatenate([bh, bl, bh], axis=1))


def move(a, b):
    if a.dtype == BF16:
        high, low = split(b)
        return dot(a, high) + dot(a, low)
    high, low = split(a)
    return dot(high, b) + dot(low, b)


def factors():
    degree = 2 * HALF_DEGREE
    z = 1.0 / RADIUS
    u = [np.poly1d([1.0]), np.poly1d([2.0, 0.0])]
    for _ in range(degree):
        u.append(np.poly1d([2.0, 0.0]) * u[-1] - u[-2])
    rest = sum((k(z) * k for k in u), np.poly1d([0.0])) / sum(k(z) ** 2 for k in u)
    scaled = np.poly1d([c * z ** (len(rest.coeffs) - 1 - i) for i, c in enumerate(rest.coeffs)])
    quotient, _ = np.polydiv((np.poly1d([1.0]) - scaled).coeffs, np.array([-1.0, 1.0]))
    roots = sorted(np.roots(quotient), key=lambda r: (abs(r.imag) < 1e-9, r.real, r.imag))
    pick = [r for i, r in enumerate(roots) if (i // 2) % 2 == 0]
    other = [r for i, r in enumerate(roots) if (i // 2) % 2 == 1]
    first = np.real(np.poly(pick))
    first = first / first[-1]
    second = np.real(np.poly(other))
    second = second / second[-1] * quotient[-1]
    return [float(c) for c in first[::-1]], [float(c) for c in second[::-1]]


def gather_kernel(
    count,
    obs_ref,
    var_ref,
    index_ref,
    dynamics_hbm,
    process_hbm,
    out_ref,
    f_ref,
    ft_ref,
    q_ref,
    perm_ref,
    perm_t_ref,
    row_ref,
    dynamics_ref,
    process_ref,
    load_sem,
    send_sem,
    recv_sem,
):
    me = lax.axis_index("tm")
    group = lax.axis_index("groups")
    gauges = obs_ref.shape[1]
    barrier = pltpu.get_barrier_semaphore()

    def greet(d, nothing):
        peer = lax.rem(me + d, count)
        pl.semaphore_signal(barrier, inc=1, device_id=(group, peer), device_id_type=MESH)
        return nothing

    lax.fori_loop(1, count, greet, 0)
    loads = [
        pltpu.make_async_copy(dynamics_hbm, dynamics_ref, load_sem.at[0]),
        pltpu.make_async_copy(process_hbm, process_ref, load_sem.at[1]),
    ]
    for load in loads:
        load.start()
    row_ref[0, :, :gauges] = obs_ref[...]
    row_ref[0, :, gauges:] = var_ref[...]
    out_ref[me] = row_ref[0]
    states = dynamics_ref.shape[0]
    perm_t = permutation(index_ref[...], states, gauges)
    perm = perm_t.T.astype(BF16)
    perm_t = perm_t.astype(BF16)
    perm_ref[...] = perm
    perm_t_ref[...] = perm_t
    pl.semaphore_wait(barrier, count - 1)

    def copy(d):
        peer = lax.rem(me + d, count)
        return pltpu.make_async_remote_copy(
            src_ref=row_ref.at[0],
            dst_ref=out_ref.at[me],
            send_sem=send_sem.at[d],
            recv_sem=recv_sem.at[d],
            device_id=(group, peer),
            device_id_type=MESH,
        )

    def start(d, nothing):
        copy(d).start()
        return nothing

    def finish(d, nothing):
        copy(d).wait()
        return nothing

    lax.fori_loop(1, count, start, 0)
    for load in loads:
        load.wait()
    f = move(move(perm, dynamics_ref[...]), perm_t)
    f_ref[0], f_ref[1] = split(f)
    ft_ref[0], ft_ref[1] = split(f.T)
    q_ref[...] = move(move(perm, process_ref[...]), perm_t)
    lax.fori_loop(1, count, finish, 0)


def kernel(
    steps,
    gathered_ref,
    f_ref,
    ft_ref,
    q_ref,
    perm_ref,
    perm_t_ref,
    filtered_ref,
    cov_ref,
    smoothed_ref,
    pred_ref,
    gain_ref,
    poly_ref,
    rows_ref,
    kept_ref,
    kept_gain_ref,
    kept_rows_ref,
    work_ref,
):
    states = q_ref.shape[0]
    gauges = gathered_ref.shape[2] // 2
    me = lax.axis_index("tm")
    rg, cg = iotas((gauges, gauges))
    eye = (rg == cg).astype(F32)
    first, second = factors()

    def gauss_jordan(s):
        work_ref[...] = s

        def pivot(k, nothing):
            m = work_ref[...]
            row = jnp.sum(jnp.where(rg == k, m, 0.0), axis=0, keepdims=True)
            col = jnp.sum(jnp.where(cg == k, m, 0.0), axis=1, keepdims=True)
            inv = 1.0 / jnp.sum(jnp.where(cg[:1] == k, row, 0.0), axis=1, keepdims=True)
            scaled = row * inv
            new = m - col * scaled
            new = jnp.where(cg == k, -col * inv, new)
            new_row = jnp.where(cg[:1] == k, inv, scaled)
            work_ref[...] = jnp.where(rg == k, new_row, new)
            return nothing

        lax.fori_loop(0, gauges, pivot, 0)
        return work_ref[...]

    def mix(coefficients, terms):
        return sum(c * m for c, m in zip(coefficients[1:], terms[1:])) + coefficients[0] * terms[0]

    def step_rows(t):
        row = gathered_ref[t]
        return row[:, :gauges], row[:, gauges:]

    def run(robust):
        pred_ref[...] = q_ref[...]
        gain_ref[0] = jnp.zeros_like(gain_ref[0])

        def gained(t, y):
            gy = dot3_t(split(jnp.broadcast_to(y, (16, gauges))), split(gain_ref[t]))[:1]
            rows_ref[t] = gy[:, :gauges]
            return gy[:, gauges:]

        def forward(t, carried):
            x, y = carried
            obs, r_row = step_rows(t)
            a = pred_ref[...]
            s = a[:gauges, :gauges] + eye * r_row
            d_row = 1.0 / jnp.sum(eye * s, axis=0, keepdims=True)
            d_col = 1.0 / jnp.sum(eye * s, axis=1, keepdims=True)
            fs = (f_ref[0], f_ref[1])
            tall = jnp.concatenate([a, jnp.broadcast_to(x, (16, states))], axis=0)
            aft = dot3(split(tall), (ft_ref[0], ft_ref[1]))
            ct = aft[:gauges]
            if not robust:
                e = eye - s * d_row
                es = split(e)
                u = dot3(es, es)
                us = split(u)
                stacked = (
                    jnp.concatenate([es[0], us[0]], axis=0),
                    jnp.concatenate([es[1], us[1]], axis=0),
                )
                eu = dot3(stacked, split(ct))
                right = [ct, eu[:gauges], eu[gauges:]]
                powers = [eye, e, u]
                left = (mix(first, right) * d_col).T
                ls, rs = split(left), split(mix(second, right))
            x = aft[states : states + 1] + gained(t, y)
            y = obs - x[:, :gauges]
            slot = jnp.where(t == me, 0, 1)
            kept_ref[slot] = a
            kept_rows_ref[slot] = jnp.broadcast_to(
                jnp.concatenate([x, y], axis=1), (8, states + gauges)
            )
            if robust:
                root_row, root_col = jnp.sqrt(d_row), jnp.sqrt(d_col)
                w = gauss_jordan(s * root_col * root_row) * root_col * root_row
                wct = full(w, ct)
                nxt = dot3(fs, split(aft[:states])) + q_ref[...]
                pred_ref[...] = nxt - full(ct.T, wct)
                gain_ref[t + 1] = jnp.concatenate([w, wct.T], axis=0)
                return x, y
            afs = split(aft[:states])
            pred_ref[...] = (
                dot3(
                    [jnp.concatenate([g, -h], axis=1) for g, h in zip(fs, ls)],
                    [jnp.concatenate([g, h], axis=0) for g, h in zip(afs, rs)],
                )
                + q_ref[...]
            )
            ps = split(mix(first, powers) * d_col)
            gain = dot3(
                (
                    jnp.concatenate([ps[0], ls[0]], axis=0),
                    jnp.concatenate([ps[1], ls[1]], axis=0),
                ),
                split(mix(second, powers)),
            )
            gain_ref[t + 1] = gain
            poly_ref[t] = s
            return x, y

        zero = jnp.zeros((1, states), F32)
        x, y = lax.fori_loop(0, steps, forward, (zero, jnp.zeros((1, gauges), F32)), unroll=4)
        gained(steps, y)

        def backward(i, carried):
            lam, worst = carried
            t = steps - 1 - i
            slot = jnp.where(t == me, 2, 3)
            hat = jnp.broadcast_to(lam, (16, states))
            hs = split(hat)
            hat = dot3(hs, (f_ref[0], f_ref[1]))[:1]
            kept_rows_ref[slot] = jnp.broadcast_to(
                jnp.concatenate([hat, rows_ref[t + 1]], axis=1), (8, states + gauges)
            )
            gain = gain_ref[t + 1]
            kept_gain_ref[jnp.where(t == me, 0, 1)] = gain[:gauges]
            fix = dot3(hs, split(gain[gauges:]))[:1]
            if not robust:
                residual = eye - dot3(split(poly_ref[t]), split(gain[:gauges]))
                worst = jnp.maximum(
                    worst, jnp.sum(residual * residual, axis=0, keepdims=True)
                )
            new = jnp.concatenate(
                [hat[:, :gauges] - rows_ref[t + 1] - fix, hat[:, gauges:]], axis=1
            )
            return new, worst

        nothing, worst = lax.fori_loop(
            0, steps, backward, (zero, jnp.zeros((1, gauges), F32)), unroll=4
        )
        return jnp.sum(worst)

    worst = run(False)

    @pl.when(jnp.logical_not(worst < RESIDUAL_LIMIT))
    def _():
        run(True)

    perm = perm_ref[...]
    a = kept_ref[0]
    w = kept_gain_ref[0]
    a_o = a[:gauges]
    r_row = step_rows(me)[1]
    s = a_o[:, :gauges] + eye * r_row
    ws = split(w)
    residual = eye - dot3(ws, split(s))
    w = w + dot(residual.astype(BF16), ws[0])
    k = dot3(split(w), split(a_o))
    cov = a - dot3(split(a[:, :gauges]), split(k))
    cov_ref[0] = move(perm_t_ref[...], move(cov, perm))
    rows, lam = kept_rows_ref[0], kept_rows_ref[2][:, :states]
    x, y = rows[:, :states], rows[:, states:]
    mean = x + dot3(split(y), split(k))
    smooth = mean - dot3(split(lam), split(cov))
    filtered_ref[...] = move(mean, perm)[:1]
    smoothed_ref[...] = move(smooth, perm)[:1]


def shards(observations, noise_var, gauge_index, dynamics, process):
    states = dynamics.shape[0]
    gauges = gauge_index.shape[0]
    steps = lax.axis_size("tm")
    vmem = pl.BlockSpec(memory_space=pltpu.VMEM)
    square = jax.ShapeDtypeStruct((states, states), BF16)
    pair = jax.ShapeDtypeStruct((2, states, states), BF16)
    prepared = pl.pallas_call(
        functools.partial(gather_kernel, steps),
        out_shape=(
            jax.ShapeDtypeStruct((steps, 1, 2 * gauges), F32),
            pair,
            pair,
            jax.ShapeDtypeStruct((states, states), F32),
            square,
            square,
        ),
        in_specs=[vmem] * 3 + [pl.BlockSpec(memory_space=pl.ANY)] * 2,
        out_specs=(vmem,) * 6,
        scratch_shapes=[
            pltpu.VMEM((1, 1, 2 * gauges), F32),
            pltpu.VMEM((states, states), F32),
            pltpu.VMEM((states, states), F32),
            pltpu.SemaphoreType.DMA((2,)),
            pltpu.SemaphoreType.DMA((steps,)),
            pltpu.SemaphoreType.DMA((steps,)),
        ],
        compiler_params=pltpu.CompilerParams(collective_id=0, has_side_effects=True, vmem_limit_bytes=56 * 1024 * 1024),
    )(observations, noise_var, gauge_index.reshape(1, gauges), dynamics, process)
    return pl.pallas_call(
        functools.partial(kernel, steps),
        out_shape=(
            jax.ShapeDtypeStruct((1, states), F32),
            jax.ShapeDtypeStruct((1, states, states), F32),
            jax.ShapeDtypeStruct((1, states), F32),
        ),
        in_specs=[vmem] * 6,
        out_specs=(vmem,) * 3,
        scratch_shapes=[
            pltpu.VMEM((states, states), F32),
            pltpu.VMEM((steps + 1, gauges + states, gauges), F32),
            pltpu.VMEM((steps, gauges, gauges), F32),
            pltpu.VMEM((steps + 1, 1, gauges), F32),
            pltpu.VMEM((2, states, states), F32),
            pltpu.VMEM((2, gauges, gauges), F32),
            pltpu.VMEM((4, 8, states + gauges), F32),
            pltpu.VMEM((gauges, gauges), F32),
        ],
        compiler_params=pltpu.CompilerParams(vmem_limit_bytes=56 * 1024 * 1024),
    )(*prepared)


def solution(mesh):
    return jax.shard_map(
        shards,
        mesh=mesh,
        in_specs=(P(("groups", "tm"), None), P(("groups", "tm"), None), P("groups"), P(), P()),
        out_specs=(
            P(("groups", "tm"), None),
            P(("groups", "tm"), None, None),
            P(("groups", "tm"), None),
        ),
        check_vma=False,
    )
```
